32 devices in a mesh: dp: 8 (over y, x, core), tensor: 4 (over z).
Axes of the slice: x: 2, y: 2, z: 4, core: 2. Of those that a mesh axis runs over, the one named last changes fastest.
Arguments:
- hidden: bfloat16 [64, 16384], P('dp'), may hold values from -6 to 6
- norm_gain: bfloat16 [16384], replicated, may hold values from 0.099609375 to 1.8984375
- query_weight: bfloat16 [16384, 16384], P('dp', 'tensor'), may hold values from -0.046875 to 0.046875
- keyval_weight: bfloat16 [16384, 8, 256], P('dp', 'tensor'), may hold values from -0.046875 to 0.046875
- output_weight: bfloat16 [16384, 16384], P('tensor', 'dp'), may hold values from -0.046875 to 0.046875
- kv_cache: bfloat16 [64, 8, 1024, 256], P('dp', 'tensor')
- cache_lengths: int32 [64], P('dp'), may hold values from 128 to 1024, as said below
- next_source: bfloat16 [128, 128, 16384], P(('dp', 'tensor')), may hold values from -0.046875 to 0.046875
- block_ids: int32 [128], P('dp'), may hold values from 0 to 127, as said below
Outputs:
- mixed: bfloat16 [64, 16384], P('dp')
- next_weight: bfloat16 [16384, 16384], P('dp', 'tensor')
The draws below stay inside these ranges and needn't reach their ends.
Inputs may be any that keep to these rules, and one draw needn't show every extreme that they name: `cache_lengths`: some row uses exactly 1024 positions. `block_ids`: a permutation; the 16 entries on one dp index name at most 2 blocks within the rows of any one dp index, and that many for some.
All inputs are finite; a program needn't handle non-finite values.
Results may differ from the reference program's by a relative error of at most 0.04.
Values may be sent and summed in bfloat16 or wider, within the bound.
A program may use at most 192 MiB of HBM per device.

```python
import jax
import jax.numpy as jnp
from jax import lax

D = 16384
KV_HEADS = 8
HEAD_DIM = 128
CACHE = 1024
BLOCK_ROWS = 128
ROWS = 64
QCOLS = 16384
NBLK = 128
GROUP_BLOCKS = 16


def draw_kv_cache(key, part):
    key = jax.random.fold_in(key, 7)
    values = jax.random.normal(key, (ROWS, KV_HEADS, CACHE, 2 * HEAD_DIM), jnp.float32)
    return values.astype(jnp.bfloat16)


def draw_cache_lengths(key, part):
    key = jax.random.fold_in(key, 5)
    length_key, row_key = jax.random.split(key)
    lengths = jax.random.randint(length_key, (ROWS,), CACHE // 8, CACHE + 1)
    chosen = jax.random.randint(row_key, (), 0, ROWS)
    return jnp.where(jnp.arange(ROWS) == chosen, CACHE, lengths).astype(jnp.int32)


def draw_block_ids(key, part):
    key = jax.random.fold_in(key, 11)
    groups = NBLK // GROUP_BLOCKS
    offset_key, order_key, shuffle_key = jax.random.split(key, 3)
    offset = jax.random.permutation(offset_key, groups).astype(jnp.int32)
    slots = jnp.arange(GROUP_BLOCKS, dtype=jnp.int32)
    target = ((slots[None, :] + offset[:, None]) % groups).reshape(-1)
    onehot = (target[:, None] == jnp.arange(groups, dtype=jnp.int32)[None, :]).astype(jnp.int32)
    arrival = jnp.sum((jnp.cumsum(onehot, axis=0) - onehot) * onehot, axis=1)
    orders = jax.vmap(lambda subkey: jax.random.permutation(subkey, GROUP_BLOCKS))(jax.random.split(order_key, groups)).astype(jnp.int32)
    numbers = (target * GROUP_BLOCKS + orders[target, arrival]).reshape(groups, GROUP_BLOCKS)
    shuffle = jax.vmap(lambda subkey: jax.random.permutation(subkey, GROUP_BLOCKS))(jax.random.split(shuffle_key, groups)).astype(jnp.int32)
    numbers = jnp.take_along_axis(numbers, shuffle, axis=1)
    return numbers.reshape(-1).astype(jnp.int32)


def steps_of(rng, dims, shards, smallest, high):
    gain = 1.0
    for dim, blocks in shards:
        steps = jax.random.uniform(jax.random.fold_in(jax.random.fold_in(rng, 6), dim), (blocks,), jnp.float32, smallest / len(shards), high / len(shards))
        gain = gain * jnp.repeat(jnp.exp(steps), dims[dim] // blocks).reshape((-1,) + (1,) * (len(dims) - 1 - dim))
    return gain


def centred(key, dims, deviation, most, cuts=(), held_as=jnp.bfloat16):
    level = steps_of(key, dims, cuts, -0.22, 0.18) if cuts else 1.0
    array = jax.random.normal(key, dims, jnp.float32) * deviation * level
    return jnp.minimum(jnp.maximum(array, -most), most).astype(held_as)


def setup_inputs(seed: int = 0) -> dict:
    streams_of = jax.random.split(jax.random.key(seed), 10)
    return {
        "hidden": centred(streams_of[0], (ROWS, D), 1.0, 6.0, ((0, 8),)),
        "norm_gain": jnp.clip(1.0 + 0.18 * jax.random.normal(streams_of[1], (D,), jnp.float32), 0.099609375, 1.8984375).astype(jnp.bfloat16),
        "query_weight": centred(streams_of[2], (D, QCOLS), D ** -0.5, 0.046875, ((0, 8), (1, 4))),
        "keyval_weight": centred(streams_of[3], (D, KV_HEADS, 2 * HEAD_DIM), D ** -0.5, 0.046875, ((0, 8), (1, 4))),
        "output_weight": centred(streams_of[4], (QCOLS, D), QCOLS ** -0.5, 0.046875, ((0, 4), (1, 8))),
        "kv_cache": draw_kv_cache(jax.random.fold_in(streams_of[9], 71), 0),
        "cache_lengths": draw_cache_lengths(jax.random.fold_in(streams_of[9], 71), 0),
        "next_source": centred(streams_of[7], (NBLK, BLOCK_ROWS, QCOLS), D ** -0.5, 0.046875, ((0, 32),)),
        "block_ids": draw_block_ids(jax.random.fold_in(streams_of[9], 71), 0),
    }


def attend(queries, new_keyval, kv_cache, cache_lengths):
    rows, groups, length, twice = kv_cache.shape
    head_dim = twice // 2
    score_scale = head_dim ** (-0.5)
    query_heads = queries.astype(jnp.float32).reshape(rows, groups, -1, head_dim)
    cache_float = kv_cache.astype(jnp.float32)
    fresh = new_keyval.astype(jnp.float32)
    scores = jnp.einsum('rjhd,rjpd->rjhp', query_heads, cache_float[..., :head_dim]) * score_scale
    visible = jnp.arange(length)[None, :] < cache_lengths[:, None]
    scores = jnp.where(visible[:, None, None, :], scores, -jnp.inf)
    self_score = jnp.einsum('rjhd,rjd->rjh', query_heads, fresh[..., :head_dim]) * score_scale
    highest = jnp.maximum(lax.optimization_barrier(jnp.max(scores, axis=-1)), self_score)
    expo = jnp.exp(scores - highest[..., None])
    self_expo = jnp.exp(self_score - highest)
    denominator = lax.optimization_barrier(jnp.sum(expo, axis=-1)) + self_expo
    weights = (expo / denominator[..., None]).astype(jnp.bfloat16)
    self_weight = (self_expo / denominator).astype(jnp.bfloat16)
    summed = jnp.einsum('rjhp,rjpd->rjhd', weights.astype(jnp.float32), cache_float[..., head_dim:])
    summed = summed + self_weight.astype(jnp.float32)[..., None] * fresh[:, :, None, head_dim:]
    return summed.astype(jnp.bfloat16).reshape(rows, -1)

def reference(hidden, norm_gain, query_weight, keyval_weight, output_weight, kv_cache, cache_lengths, next_source, block_ids):
    stream = hidden.astype(jnp.float32)
    meansq = lax.optimization_barrier(jnp.mean(stream * stream, axis=-1, keepdims=True))
    normed = (stream * jax.lax.rsqrt(meansq + 1e-05) * norm_gain.astype(jnp.float32)).astype(jnp.bfloat16)
    queries = jnp.dot(normed, query_weight, preferred_element_type=jnp.float32).astype(jnp.bfloat16)
    flat_kv = keyval_weight.reshape(keyval_weight.shape[0], -1)
    new_keyval = jnp.dot(normed, flat_kv, preferred_element_type=jnp.float32).astype(jnp.bfloat16)
    new_keyval = new_keyval.reshape(hidden.shape[0], KV_HEADS, 2 * HEAD_DIM)
    heads_out = attend(queries, new_keyval, kv_cache, cache_lengths)
    attention = jnp.dot(heads_out, output_weight, preferred_element_type=jnp.float32).astype(jnp.bfloat16)
    mixed = (stream + attention.astype(jnp.float32)).astype(jnp.bfloat16)
    placed = jnp.zeros((NBLK, BLOCK_ROWS, QCOLS), jnp.bfloat16).at[block_ids].set(next_source)
    return (mixed, placed.reshape(D, QCOLS))
```

```python
import functools

import jax
import jax.numpy as jnp
from jax import lax
from jax.experimental import pallas as pl
from jax.experimental.pallas import tpu as pltpu
from jax.sharding import PartitionSpec as P


def attend(queries, new_keyval, kv_cache, cache_lengths):
    rows, groups, length, twice = kv_cache.shape
    head_dim = twice // 2
    score_scale = head_dim ** (-0.5)
    query_heads = queries.reshape(rows, groups, -1, head_dim)
    scores = (
        jnp.einsum(
            "rjhd,rjpd->rjhp",
            query_heads,
            kv_cache[..., :head_dim],
            preferred_element_type=jnp.float32,
        )
        * score_scale
    )
    visible = jnp.arange(length)[None, :] < cache_lengths[:, None]
    scores = jnp.where(visible[:, None, None, :], scores, -jnp.inf)
    self_score = (
        jnp.einsum(
            "rjhd,rjd->rjh",
            query_heads,
            new_keyval[..., :head_dim],
            preferred_element_type=jnp.float32,
        )
        * score_scale
    )
    highest = jnp.maximum(jnp.max(scores, axis=-1), self_score)
    expo = jnp.exp(scores - highest[..., None])
    self_expo = jnp.exp(self_score - highest)
    denominator = jnp.sum(expo, axis=-1) + self_expo
    weights = (expo / denominator[..., None]).astype(jnp.bfloat16)
    self_weight = (self_expo / denominator).astype(jnp.bfloat16)
    summed = jnp.einsum(
        "rjhp,rjpd->rjhd", weights, kv_cache[..., head_dim:], preferred_element_type=jnp.float32
    )
    summed = summed + self_weight.astype(jnp.float32)[..., None] * new_keyval[
        :, :, None, head_dim:
    ].astype(jnp.float32)
    return summed.astype(jnp.bfloat16).reshape(rows, -1)


CHUNK = 16
EARLY = 48
AHEAD = 3


def route_kernel(
    dp_count,
    tensor_count,
    early_chunks,
    send_index,
    source,
    early,
    summed,
    incoming,
    attention,
    *scratch,
):
    blocks, block_rows, _ = source.shape
    columns = incoming.shape[2]
    capacity = incoming.shape[0] // dp_count
    chunks = block_rows // CHUNK
    late = chunks - early_chunks
    held = scratch[:chunks]
    ordered = scratch[chunks : 2 * chunks]
    (
        early_sem,
        own_sem,
        tensor_send,
        tensor_recv,
        place_sem,
        dp_send,
        dp_recv,
        att_sem,
        att_send,
        att_recv,
    ) = scratch[2 * chunks :]
    me = lax.axis_index("dp")
    mine = lax.axis_index("tensor")

    def dp_peer(step):
        return lax.rem(me + step, dp_count)

    def tensor_peer(step):
        return lax.rem(mine + step, tensor_count)

    def tile(chunk, owner):
        return source.at[
            :,
            pl.ds(chunk * CHUNK, CHUNK),
            pl.ds(pl.multiple_of(owner * columns, 128), columns),
        ]

    def early_copy(chunk):
        return pltpu.make_async_copy(
            early.at[:, pl.ds(chunk * CHUNK, CHUNK), :], held[chunk], early_sem.at[chunk]
        )

    def own_copy(chunk):
        return pltpu.make_async_copy(
            tile(chunk, mine),
            held[chunk].at[pl.ds(mine * blocks, blocks)],
            own_sem.at[chunk - early_chunks],
        )

    def tensor_copy(chunk, step):
        return pltpu.make_async_remote_copy(
            src_ref=tile(chunk, tensor_peer(step)),
            dst_ref=held[chunk].at[pl.ds(mine * blocks, blocks)],
            send_sem=tensor_send.at[chunk - early_chunks, step],
            recv_sem=tensor_recv.at[chunk - early_chunks, step],
            device_id={"tensor": tensor_peer(step)},
            device_id_type=pl.DeviceIdType.MESH,
        )

    def place(chunk):
        return incoming.at[pl.ds(me * capacity, capacity), pl.ds(chunk * CHUNK, CHUNK), :]

    def place_copy(chunk):
        return pltpu.make_async_copy(
            ordered[chunk].at[pl.ds(me * capacity, capacity)], place(chunk), place_sem.at[chunk]
        )

    def dp_copy(chunk, step):
        return pltpu.make_async_remote_copy(
            src_ref=ordered[chunk].at[pl.ds(dp_peer(step) * capacity, capacity)],
            dst_ref=place(chunk),
            send_sem=dp_send.at[chunk, step],
            recv_sem=dp_recv.at[chunk, step],
            device_id={"dp": dp_peer(step)},
            device_id_type=pl.DeviceIdType.MESH,
        )

    def att_copy(step):
        return pltpu.make_async_remote_copy(
            src_ref=summed.at[dp_peer(step)],
            dst_ref=attention.at[me],
            send_sem=att_send.at[step],
            recv_sem=att_recv.at[step],
            device_id={"dp": dp_peer(step)},
            device_id_type=pl.DeviceIdType.MESH,
        )

    def start_tensor(chunk):
        for step in range(1, tensor_count):
            tensor_copy(chunk, step).start()
        own_copy(chunk).start()

    barrier = pltpu.get_barrier_semaphore()
    for step in range(1, dp_count):
        pl.semaphore_signal(
            barrier, inc=1, device_id={"dp": dp_peer(step)}, device_id_type=pl.DeviceIdType.MESH
        )
    for step in range(1, tensor_count):
        pl.semaphore_signal(
            barrier,
            inc=1,
            device_id={"tensor": tensor_peer(step)},
            device_id_type=pl.DeviceIdType.MESH,
        )
    pl.semaphore_wait(barrier, dp_count - 1 + tensor_count - 1)

    for chunk in range(early_chunks, min(early_chunks + AHEAD, chunks)):
        start_tensor(chunk)
    for chunk in range(early_chunks):
        early_copy(chunk).start()
    att_own = pltpu.make_async_copy(summed.at[me], attention.at[me], att_sem)
    att_own.start()
    lax.fori_loop(1, dp_count, lambda step, _: (att_copy(step).start(), None)[1], None)

    for chunk in range(chunks):
        if chunk < early_chunks:
            early_copy(chunk).wait()
        else:
            own_copy(chunk).wait()
            for step in range(1, tensor_count):
                tensor_copy(chunk, step).wait_recv()
            if chunk + AHEAD < chunks:
                start_tensor(chunk + AHEAD)

        def reorder(slot, _, chunk=chunk):
            ordered[chunk][slot] = held[chunk][send_index[slot]]

        lax.fori_loop(0, dp_count * capacity, reorder, None)
        lax.fori_loop(
            1, dp_count, lambda step, _, chunk=chunk: (dp_copy(chunk, step).start(), None)[1], None
        )
        place_copy(chunk).start()

    att_own.wait()
    lax.fori_loop(1, dp_count, lambda step, _: (att_copy(step).wait(), None)[1], None)
    for chunk in range(chunks):
        if chunk >= early_chunks:
            for step in range(1, tensor_count):
                tensor_copy(chunk, step).wait_send()
        place_copy(chunk).wait()
        lax.fori_loop(
            1, dp_count, lambda step, _, chunk=chunk: (dp_copy(chunk, step).wait(), None)[1], None
        )


def route(send_index, source, early, summed, dp_count, tensor_count, capacity):
    blocks, block_rows, width = source.shape
    group_size = blocks * tensor_count
    columns = width // tensor_count
    chunks = block_rows // CHUNK
    early_chunks = early.shape[1] // CHUNK
    late = chunks - early_chunks
    slots = dp_count * capacity
    anywhere = pl.BlockSpec(memory_space=pl.ANY)
    dma = pltpu.SemaphoreType.DMA
    return pl.pallas_call(
        functools.partial(route_kernel, dp_count, tensor_count, early_chunks),
        out_shape=(
            jax.ShapeDtypeStruct((slots, block_rows, columns), jnp.bfloat16),
            jax.ShapeDtypeStruct(summed.shape, summed.dtype),
        ),
        in_specs=[pl.BlockSpec(memory_space=pltpu.SMEM), anywhere, anywhere, anywhere],
        out_specs=(anywhere, anywhere),
        scratch_shapes=[pltpu.VMEM((group_size, CHUNK, columns), jnp.bfloat16)] * chunks
        + [pltpu.VMEM((slots, CHUNK, columns), jnp.bfloat16)] * chunks
        + [
            dma((early_chunks,)),
            dma((late,)),
            dma((late, tensor_count)),
            dma((late, tensor_count)),
            dma((chunks,)),
            dma((chunks, dp_count)),
            dma((chunks, dp_count)),
            dma,
            dma((dp_count,)),
            dma((dp_count,)),
        ],
        compiler_params=pltpu.CompilerParams(
            collective_id=0, has_side_effects=True, vmem_limit_bytes=44 * 1024 * 1024
        ),
        cost_estimate=pl.CostEstimate(
            flops=0, bytes_accessed=4 * slots * block_rows * columns, transcendentals=0
        ),
        name="route",
    )(send_index, source, early, summed)


def put_kernel(slot_of, block, out):
    out[...] = block[...]


def put(slot_of, incoming):
    group_size = slot_of.shape[0]
    _, block_rows, columns = incoming.shape
    return pl.pallas_call(
        put_kernel,
        out_shape=jax.ShapeDtypeStruct((group_size, block_rows, columns), jnp.bfloat16),
        grid_spec=pltpu.PrefetchScalarGridSpec(
            num_scalar_prefetch=1,
            grid=(group_size,),
            in_specs=[
                pl.BlockSpec((1, block_rows, columns), lambda place, slots: (slots[place], 0, 0))
            ],
            out_specs=pl.BlockSpec((1, block_rows, columns), lambda place, slots: (place, 0, 0)),
        ),
        compiler_params=pltpu.CompilerParams(vmem_limit_bytes=16 * 1024 * 1024),
        name="put",
    )(slot_of, incoming)


def routing_tables(block_ids, dp_count):
    group_size = block_ids.shape[0]
    capacity = max(1, group_size // dp_count)
    me = lax.axis_index("dp")
    numbers = lax.all_gather(block_ids, "dp", axis=0)
    target = numbers // group_size
    earlier = jnp.arange(group_size)[:, None] > jnp.arange(group_size)[None, :]
    same = (target[:, :, None] == target[:, None, :]) & earlier[None]
    arrival = jnp.sum(same.astype(jnp.int32), axis=2)
    my_slot = (target * capacity + arrival)[me]
    slots = jnp.arange(dp_count * capacity, dtype=jnp.int32)
    order = jnp.arange(group_size, dtype=jnp.int32)
    send_index = jnp.sum(
        jnp.where(slots[:, None] == my_slot[None, :], order[None, :], 0), axis=1, dtype=jnp.int32
    )
    from_slot = jnp.arange(dp_count, dtype=jnp.int32)[:, None] * capacity + arrival
    wanted = numbers.reshape(-1)[None, :] == (me * group_size + order)[:, None]
    slot_of = jnp.sum(
        jnp.where(wanted, from_slot.reshape(-1)[None, :], 0), axis=1, dtype=jnp.int32
    )
    return send_index, slot_of, capacity


def on_device(
    hidden,
    norm_gain,
    query_weight,
    keyval_weight,
    output_weight,
    kv_cache,
    cache_lengths,
    next_source,
    block_ids,
):
    rows_dev = hidden.shape[0]
    dp_count = lax.axis_size("dp")
    tensor_count = lax.axis_size("tensor")
    blocks, _, width = next_source.shape
    early = lax.all_to_all(
        next_source[:, :EARLY]
        .reshape(blocks, EARLY, tensor_count, width // tensor_count)
        .transpose(2, 0, 1, 3),
        "tensor",
        split_axis=0,
        concat_axis=0,
        tiled=True,
    ).reshape(tensor_count * blocks, EARLY, width // tensor_count)
    send_index, slot_of, capacity = routing_tables(block_ids, dp_count)
    stream = hidden.astype(jnp.float32)
    meansq = jnp.mean(stream * stream, axis=-1, keepdims=True)
    normed = (stream * lax.rsqrt(meansq + 1e-05) * norm_gain.astype(jnp.float32)).astype(
        jnp.bfloat16
    )
    pieces = lax.all_to_all(normed, "dp", split_axis=1, concat_axis=0, tiled=True)
    flat_kv = keyval_weight.reshape(keyval_weight.shape[0], -1)
    query_cols = query_weight.shape[1]
    projected = lax.psum_scatter(
        jnp.concatenate(
            [
                jnp.dot(pieces, query_weight, preferred_element_type=jnp.float32),
                jnp.dot(pieces, flat_kv, preferred_element_type=jnp.float32),
            ],
            axis=1,
        ).astype(jnp.bfloat16),
        "dp",
        scatter_dimension=0,
        tiled=True,
    ).astype(jnp.float32)
    queries = projected[:, :query_cols].astype(jnp.bfloat16)
    new_keyval = (
        projected[:, query_cols:]
        .astype(jnp.bfloat16)
        .reshape(rows_dev, keyval_weight.shape[1], keyval_weight.shape[2])
    )
    heads_out = attend(queries, new_keyval, kv_cache, cache_lengths)
    partial_out = jnp.dot(
        lax.all_gather(heads_out, "dp", axis=0, tiled=True),
        output_weight,
        preferred_element_type=jnp.float32,
    )
    summed = lax.psum(partial_out.astype(jnp.bfloat16), "tensor").astype(jnp.float32)
    incoming, attention = route(
        send_index,
        next_source,
        early,
        summed.reshape(dp_count, rows_dev, -1),
        dp_count,
        tensor_count,
        capacity,
    )
    next_weight = put(slot_of, incoming).reshape(-1, incoming.shape[2])
    attention = attention.transpose(1, 0, 2).reshape(rows_dev, -1)
    mixed = (stream + attention).astype(jnp.bfloat16)
    return (mixed, next_weight)


def solution(mesh):
    return jax.shard_map(
        on_device,
        mesh=mesh,
        in_specs=(
            P("dp", None),
            P(),
            P("dp", "tensor"),
            P("dp", "tensor", None),
            P("tensor", "dp"),
            P("dp", "tensor", None, None),
            P("dp"),
            P(("dp", "tensor"), None, None),
            P("dp"),
        ),
        out_specs=(P("dp", None), P("dp", "tensor")),
        check_vma=False,
    )
```

```python
import functools

import jax
import jax.numpy as jnp
from jax import lax
from jax.experimental import pallas as pl
from jax.experimental.pallas import tpu as pltpu
from jax.sharding import PartitionSpec as P


def attend(queries, new_keyval, kv_cache, cache_lengths):
    rows, groups, length, twice = kv_cache.shape
    head_dim = twice // 2
    score_scale = head_dim ** (-0.5)
    query_heads = queries.reshape(rows, groups, -1, head_dim)
    scores = (
        jnp.einsum(
            "rjhd,rjpd->rjhp",
            query_heads,
            kv_cache[..., :head_dim],
            preferred_element_type=jnp.float32,
        )
        * score_scale
    )
    visible = jnp.arange(length)[None, :] < cache_lengths[:, None]
    scores = jnp.where(visible[:, None, None, :], scores, -jnp.inf)
    self_score = (
        jnp.einsum(
            "rjhd,rjd->rjh",
            query_heads,
            new_keyval[..., :head_dim],
            preferred_element_type=jnp.float32,
        )
        * score_scale
    )
    highest = jnp.maximum(jnp.max(scores, axis=-1), self_score)
    expo = jnp.exp(scores - highest[..., None])
    self_expo = jnp.exp(self_score - highest)
    denominator = jnp.sum(expo, axis=-1) + self_expo
    weights = (expo / denominator[..., None]).astype(jnp.bfloat16)
    self_weight = (self_expo / denominator).astype(jnp.bfloat16)
    summed = jnp.einsum(
        "rjhp,rjpd->rjhd", weights, kv_cache[..., head_dim:], preferred_element_type=jnp.float32
    )
    summed = summed + self_weight.astype(jnp.float32)[..., None] * new_keyval[
        :, :, None, head_dim:
    ].astype(jnp.float32)
    return summed.astype(jnp.bfloat16).reshape(rows, -1)


CHUNK = 16
EARLY = 32
AHEAD = 3
TAIL_PARTS = 4


def chunk_list(block_rows, early_rows, columns):
    parts = [(row, 0, columns) for row in range(0, block_rows - CHUNK, CHUNK)]
    width = columns // TAIL_PARTS
    parts += [(block_rows - CHUNK, width * part, width) for part in range(TAIL_PARTS)]
    return parts, early_rows // CHUNK


def route_kernel(
    dp_count,
    tensor_count,
    send_index,
    source,
    early,
    partial,
    incoming,
    attention,
    *scratch,
):
    blocks, block_rows, _ = source.shape
    columns = incoming.shape[2]
    capacity = incoming.shape[0] // dp_count
    parts, early_chunks = chunk_list(block_rows, early.shape[1], columns)
    chunks = len(parts)
    held = scratch[:chunks]
    ordered = scratch[chunks : 2 * chunks]
    (
        gathered,
        outgoing,
        arrived,
        total,
        early_sem,
        own_sem,
        tensor_send,
        tensor_recv,
        place_sem,
        dp_send,
        dp_recv,
        att_sem,
        att_send,
        att_recv,
        reduce_send,
        reduce_recv,
        share_sem,
        share_send,
        share_recv,
    ) = scratch[2 * chunks :]
    share = dp_count // tensor_count
    me = lax.axis_index("dp")
    mine = lax.axis_index("tensor")

    def dp_peer(step):
        return lax.rem(me + step, dp_count)

    def tensor_peer(step):
        return lax.rem(mine + step, tensor_count)

    def tile(chunk, owner):
        row, column, width = parts[chunk]
        return source.at[
            :,
            pl.ds(row, CHUNK),
            pl.ds(pl.multiple_of(owner * columns + column, 128), width),
        ]

    def early_copy(chunk):
        return pltpu.make_async_copy(
            early.at[:, pl.ds(parts[chunk][0], CHUNK), :], held[chunk], early_sem.at[chunk]
        )

    def own_copy(chunk):
        return pltpu.make_async_copy(
            tile(chunk, mine),
            held[chunk].at[pl.ds(mine * blocks, blocks)],
            own_sem.at[chunk - early_chunks],
        )

    def tensor_copy(chunk, step):
        return pltpu.make_async_remote_copy(
            src_ref=tile(chunk, tensor_peer(step)),
            dst_ref=held[chunk].at[pl.ds(mine * blocks, blocks)],
            send_sem=tensor_send.at[chunk - early_chunks, step],
            recv_sem=tensor_recv.at[chunk - early_chunks, step],
            device_id={"tensor": tensor_peer(step)},
            device_id_type=pl.DeviceIdType.MESH,
        )

    def place(chunk):
        row, column, width = parts[chunk]
        return incoming.at[
            pl.ds(me * capacity, capacity), pl.ds(row, CHUNK), pl.ds(column, width)
        ]

    def place_copy(chunk):
        return pltpu.make_async_copy(
            ordered[chunk].at[pl.ds(me * capacity, capacity)], place(chunk), place_sem.at[chunk]
        )

    def dp_copy(chunk, step):
        return pltpu.make_async_remote_copy(
            src_ref=ordered[chunk].at[pl.ds(dp_peer(step) * capacity, capacity)],
            dst_ref=place(chunk),
            send_sem=dp_send.at[chunk, step],
            recv_sem=dp_recv.at[chunk, step],
            device_id={"dp": dp_peer(step)},
            device_id_type=pl.DeviceIdType.MESH,
        )

    def att_copy(step):
        return pltpu.make_async_remote_copy(
            src_ref=partial.at[dp_peer(step)],
            dst_ref=gathered.at[me],
            send_sem=att_send.at[step],
            recv_sem=att_recv.at[step],
            device_id={"dp": dp_peer(step)},
            device_id_type=pl.DeviceIdType.MESH,
        )

    def reduce_copy(step):
        return pltpu.make_async_remote_copy(
            src_ref=outgoing.at[tensor_peer(step)],
            dst_ref=arrived.at[mine],
            send_sem=reduce_send.at[step],
            recv_sem=reduce_recv.at[step],
            device_id={"tensor": tensor_peer(step)},
            device_id_type=pl.DeviceIdType.MESH,
        )

    def share_copy(step):
        return pltpu.make_async_remote_copy(
            src_ref=total,
            dst_ref=attention.at[mine],
            send_sem=share_send.at[step],
            recv_sem=share_recv.at[step],
            device_id={"tensor": tensor_peer(step)},
            device_id_type=pl.DeviceIdType.MESH,
        )

    def start_reduce():
        att_own.wait()
        lax.fori_loop(1, dp_count, lambda step, _: (att_copy(step).wait(), None)[1], None)
        for owner in range(tensor_count):
            rows = gathered[owner * share : (owner + 1) * share]
            outgoing[owner] = rows.reshape(outgoing.shape[1:]).astype(outgoing.dtype)
        for step in range(1, tensor_count):
            reduce_copy(step).start()

    def start_share():
        for step in range(1, tensor_count):
            reduce_copy(step).wait()
        value = outgoing[mine].astype(jnp.float32)
        for step in range(1, tensor_count):
            value += arrived[tensor_peer(step)].astype(jnp.float32)
        total[...] = value.astype(total.dtype)
        for step in range(1, tensor_count):
            share_copy(step).start()
        share_own.start()

    def start_tensor(chunk):
        for step in range(1, tensor_count):
            tensor_copy(chunk, step).start()
        own_copy(chunk).start()

    barrier = pltpu.get_barrier_semaphore()
    for step in range(1, dp_count):
        pl.semaphore_signal(
            barrier, inc=1, device_id={"dp": dp_peer(step)}, device_id_type=pl.DeviceIdType.MESH
        )
    for step in range(1, tensor_count):
        pl.semaphore_signal(
            barrier,
            inc=1,
            device_id={"tensor": tensor_peer(step)},
            device_id_type=pl.DeviceIdType.MESH,
        )
    pl.semaphore_wait(barrier, dp_count - 1 + tensor_count - 1)

    for chunk in range(early_chunks, min(early_chunks + AHEAD, chunks)):
        start_tensor(chunk)
    for chunk in range(early_chunks):
        early_copy(chunk).start()
    att_own = pltpu.make_async_copy(partial.at[me], gathered.at[me], att_sem)
    share_own = pltpu.make_async_copy(total, attention.at[mine], share_sem)
    att_own.start()
    lax.fori_loop(1, dp_count, lambda step, _: (att_copy(step).start(), None)[1], None)

    for chunk in range(chunks):
        if chunk == early_chunks:
            start_reduce()
        if chunk == early_chunks + AHEAD:
            start_share()
        if chunk < early_chunks:
            early_copy(chunk).wait()
        else:
            own_copy(chunk).wait()
            for step in range(1, tensor_count):
                tensor_copy(chunk, step).wait_recv()
            if chunk + AHEAD < chunks:
                start_tensor(chunk + AHEAD)

        def reorder(slot, _, chunk=chunk):
            ordered[chunk][slot] = held[chunk][send_index[slot]]

        lax.fori_loop(0, dp_count * capacity, reorder, None)
        lax.fori_loop(
            1, dp_count, lambda step, _, chunk=chunk: (dp_copy(chunk, step).start(), None)[1], None
        )
        place_copy(chunk).start()

    share_own.wait()
    for step in range(1, tensor_count):
        share_copy(step).wait()
    for chunk in range(chunks):
        if chunk >= early_chunks:
            for step in range(1, tensor_count):
                tensor_copy(chunk, step).wait_send()
        place_copy(chunk).wait()
        lax.fori_loop(
            1, dp_count, lambda step, _, chunk=chunk: (dp_copy(chunk, step).wait(), None)[1], None
        )


def route(send_index, source, early, partial, dp_count, tensor_count, capacity):
    blocks, block_rows, width = source.shape
    group_size = blocks * tensor_count
    columns = width // tensor_count
    parts, early_chunks = chunk_list(block_rows, early.shape[1], columns)
    chunks = len(parts)
    late = chunks - early_chunks
    slots = dp_count * capacity
    shared = (dp_count // tensor_count * partial.shape[1], partial.shape[2])
    exchanged = (tensor_count, *shared)
    anywhere = pl.BlockSpec(memory_space=pl.ANY)
    dma = pltpu.SemaphoreType.DMA
    return pl.pallas_call(
        functools.partial(route_kernel, dp_count, tensor_count),
        out_shape=(
            jax.ShapeDtypeStruct((slots, block_rows, columns), jnp.bfloat16),
            jax.ShapeDtypeStruct(exchanged, jnp.bfloat16),
        ),
        in_specs=[pl.BlockSpec(memory_space=pltpu.SMEM), anywhere, anywhere, anywhere],
        out_specs=(anywhere, anywhere),
        scratch_shapes=[
            pltpu.VMEM((group_size, CHUNK, part[2]), jnp.bfloat16) for part in parts
        ]
        + [pltpu.VMEM((slots, CHUNK, part[2]), jnp.bfloat16) for part in parts]
        + [
            pltpu.VMEM(partial.shape, jnp.float32),
            pltpu.VMEM(exchanged, jnp.bfloat16),
            pltpu.VMEM(exchanged, jnp.bfloat16),
            pltpu.VMEM(shared, jnp.bfloat16),
            dma((early_chunks,)),
            dma((late,)),
            dma((late, tensor_count)),
            dma((late, tensor_count)),
            dma((chunks,)),
            dma((chunks, dp_count)),
            dma((chunks, dp_count)),
            dma,
            dma((dp_count,)),
            dma((dp_count,)),
            dma((tensor_count,)),
            dma((tensor_count,)),
            dma,
            dma((tensor_count,)),
            dma((tensor_count,)),
        ],
        compiler_params=pltpu.CompilerParams(
            collective_id=0, has_side_effects=True, vmem_limit_bytes=44 * 1024 * 1024
        ),
        cost_estimate=pl.CostEstimate(
            flops=0, bytes_accessed=4 * slots * block_rows * columns, transcendentals=0
        ),
        name="route",
    )(send_index, source, early, partial)


def put_kernel(slot_of, block, out):
    out[...] = block[...]


def put(slot_of, incoming):
    group_size = slot_of.shape[0]
    _, block_rows, columns = incoming.shape
    return pl.pallas_call(
        put_kernel,
        out_shape=jax.ShapeDtypeStruct((group_size, block_rows, columns), jnp.bfloat16),
        grid_spec=pltpu.PrefetchScalarGridSpec(
            num_scalar_prefetch=1,
            grid=(group_size,),
            in_specs=[
                pl.BlockSpec((1, block_rows, columns), lambda place, slots: (slots[place], 0, 0))
            ],
            out_specs=pl.BlockSpec((1, block_rows, columns), lambda place, slots: (place, 0, 0)),
        ),
        compiler_params=pltpu.CompilerParams(vmem_limit_bytes=52 * 1024 * 1024),
        name="put",
    )(slot_of, incoming)


def routing_tables(block_ids, dp_count):
    group_size = block_ids.shape[0]
    capacity = max(1, group_size // dp_count)
    me = lax.axis_index("dp")
    numbers = lax.all_gather(block_ids, "dp", axis=0)
    target = numbers // group_size
    earlier = jnp.arange(group_size)[:, None] > jnp.arange(group_size)[None, :]
    same = (target[:, :, None] == target[:, None, :]) & earlier[None]
    arrival = jnp.sum(same.astype(jnp.int32), axis=2)
    my_slot = (target * capacity + arrival)[me]
    slots = jnp.arange(dp_count * capacity, dtype=jnp.int32)
    order = jnp.arange(group_size, dtype=jnp.int32)
    send_index = jnp.sum(
        jnp.where(slots[:, None] == my_slot[None, :], order[None, :], 0), axis=1, dtype=jnp.int32
    )
    from_slot = jnp.arange(dp_count, dtype=jnp.int32)[:, None] * capacity + arrival
    wanted = numbers.reshape(-1)[None, :] == (me * group_size + order)[:, None]
    slot_of = jnp.sum(
        jnp.where(wanted, from_slot.reshape(-1)[None, :], 0), axis=1, dtype=jnp.int32
    )
    return send_index, slot_of, capacity


def on_device(
    hidden,
    norm_gain,
    query_weight,
    keyval_weight,
    output_weight,
    kv_cache,
    cache_lengths,
    next_source,
    block_ids,
):
    rows_dev = hidden.shape[0]
    dp_count = lax.axis_size("dp")
    tensor_count = lax.axis_size("tensor")
    blocks, _, width = next_source.shape
    early = lax.all_to_all(
        next_source[:, :EARLY]
        .reshape(blocks, EARLY, tensor_count, width // tensor_count)
        .transpose(2, 0, 1, 3),
        "tensor",
        split_axis=0,
        concat_axis=0,
        tiled=True,
    ).reshape(tensor_count * blocks, EARLY, width // tensor_count)
    send_index, slot_of, capacity = routing_tables(block_ids, dp_count)
    stream = hidden.astype(jnp.float32)
    meansq = jnp.mean(stream * stream, axis=-1, keepdims=True)
    normed = (stream * lax.rsqrt(meansq + 1e-05) * norm_gain.astype(jnp.float32)).astype(
        jnp.bfloat16
    )
    pieces = lax.all_to_all(normed, "dp", split_axis=1, concat_axis=0, tiled=True)
    flat_kv = keyval_weight.reshape(keyval_weight.shape[0], -1)
    query_cols = query_weight.shape[1]
    projected = lax.psum_scatter(
        jnp.concatenate(
            [
                jnp.dot(pieces, query_weight, preferred_element_type=jnp.float32),
                jnp.dot(pieces, flat_kv, preferred_element_type=jnp.float32),
            ],
            axis=1,
        ).astype(jnp.bfloat16),
        "dp",
        scatter_dimension=0,
        tiled=True,
    ).astype(jnp.float32)
    queries = projected[:, :query_cols].astype(jnp.bfloat16)
    new_keyval = (
        projected[:, query_cols:]
        .astype(jnp.bfloat16)
        .reshape(rows_dev, keyval_weight.shape[1], keyval_weight.shape[2])
    )
    heads_out = attend(queries, new_keyval, kv_cache, cache_lengths)
    partial_out = jnp.dot(
        lax.all_gather(heads_out, "dp", axis=0, tiled=True),
        output_weight,
        preferred_element_type=jnp.float32,
    )
    incoming, attention = route(
        send_index,
        next_source,
        early,
        partial_out.reshape(dp_count, rows_dev, -1),
        dp_count,
        tensor_count,
        capacity,
    )
    next_weight = put(slot_of, incoming).reshape(-1, incoming.shape[2])
    attention = attention.reshape(dp_count, rows_dev, -1).transpose(1, 0, 2)
    attention = attention.reshape(rows_dev, -1).astype(jnp.float32)
    mixed = (stream + attention).astype(jnp.bfloat16)
    return (mixed, next_weight)


def solution(mesh):
    return jax.shard_map(
        on_device,
        mesh=mesh,
        in_specs=(
            P("dp", None),
            P(),
            P("dp", "tensor"),
            P("dp", "tensor", None),
            P("tensor", "dp"),
            P("dp", "tensor", None, None),
            P("dp"),
            P(("dp", "tensor"), None, None),
            P("dp"),
        ),
        out_specs=(P("dp", None), P("dp", "tensor")),
        check_vma=False,
    )
```

```python
import functools

import jax
import jax.numpy as jnp
from jax import lax
from jax.experimental import pallas as pl
from jax.experimental.pallas import tpu as pltpu
from jax.sharding import PartitionSpec as P


def attend(queries, new_keyval, kv_cache, cache_lengths):
    rows, groups, length, twice = kv_cache.shape
    head_dim = twice // 2
    score_scale = head_dim ** (-0.5)
    query_heads = queries.reshape(rows, groups, -1, head_dim)
    scores = (
        jnp.einsum(
            "rjhd,rjpd->rjhp",
            query_heads,
            kv_cache[..., :head_dim],
            preferred_element_type=jnp.float32,
        )
        * score_scale
    )
    visible = jnp.arange(length)[None, :] < cache_lengths[:, None]
    scores = jnp.where(visible[:, None, None, :], scores, -jnp.inf)
    self_score = (
        jnp.einsum(
            "rjhd,rjd->rjh",
            query_heads,
            new_keyval[..., :head_dim],
            preferred_element_type=jnp.float32,
        )
        * score_scale
    )
    highest = jnp.maximum(jnp.max(scores, axis=-1), self_score)
    expo = jnp.exp(scores - highest[..., None])
    self_expo = jnp.exp(self_score - highest)
    denominator = jnp.sum(expo, axis=-1) + self_expo
    weights = (expo / denominator[..., None]).astype(jnp.bfloat16)
    self_weight = (self_expo / denominator).astype(jnp.bfloat16)
    summed = jnp.einsum(
        "rjhp,rjpd->rjhd", weights, kv_cache[..., head_dim:], preferred_element_type=jnp.float32
    )
    summed = summed + self_weight.astype(jnp.float32)[..., None] * new_keyval[
        :, :, None, head_dim:
    ].astype(jnp.float32)
    return summed.astype(jnp.bfloat16).reshape(rows, -1)


CHUNK = 16
EARLY = 32
AHEAD = 3
TAIL_PARTS = 4


def chunk_list(block_rows, early_rows, columns):
    parts = [(row, 0, columns) for row in range(0, block_rows - CHUNK, CHUNK)]
    width = columns // TAIL_PARTS
    parts += [(block_rows - CHUNK, width * part, width) for part in range(TAIL_PARTS)]
    return parts, early_rows // CHUNK


def route_kernel(
    dp_count,
    tensor_count,
    send_index,
    source,
    early,
    partial,
    incoming,
    attention,
    *scratch,
):
    blocks, block_rows, _ = source.shape
    columns = incoming.shape[2]
    capacity = incoming.shape[0] // dp_count
    parts, early_chunks = chunk_list(block_rows, early.shape[1], columns)
    chunks = len(parts)
    held = scratch[:chunks]
    ordered = scratch[chunks : 2 * chunks]
    (
        gathered,
        outgoing,
        arrived,
        total,
        early_sem,
        own_sem,
        tensor_send,
        tensor_recv,
        place_sem,
        dp_send,
        dp_recv,
        att_sem,
        att_send,
        att_recv,
        reduce_send,
        reduce_recv,
        share_sem,
        share_send,
        share_recv,
    ) = scratch[2 * chunks :]
    share = dp_count // tensor_count
    me = lax.axis_index("dp")
    mine = lax.axis_index("tensor")

    def dp_peer(step):
        return lax.rem(me + step, dp_count)

    def tensor_peer(step):
        return lax.rem(mine + step, tensor_count)

    def tile(chunk, owner):
        row, column, width = parts[chunk]
        return source.at[
            :,
            pl.ds(row, CHUNK),
            pl.ds(pl.multiple_of(owner * columns + column, 128), width),
        ]

    def early_copy(chunk):
        return pltpu.make_async_copy(
            early.at[:, pl.ds(parts[chunk][0], CHUNK), :], held[chunk], early_sem.at[chunk]
        )

    def own_copy(chunk):
        return pltpu.make_async_copy(
            tile(chunk, mine),
            held[chunk].at[pl.ds(mine * blocks, blocks)],
            own_sem.at[chunk - early_chunks],
        )

    def tensor_copy(chunk, step):
        return pltpu.make_async_remote_copy(
            src_ref=tile(chunk, tensor_peer(step)),
            dst_ref=held[chunk].at[pl.ds(mine * blocks, blocks)],
            send_sem=tensor_send.at[chunk - early_chunks, step],
            recv_sem=tensor_recv.at[chunk - early_chunks, step],
            device_id={"tensor": tensor_peer(step)},
            device_id_type=pl.DeviceIdType.MESH,
        )

    def place(chunk):
        row, column, width = parts[chunk]
        return incoming.at[
            pl.ds(me * capacity, capacity), pl.ds(row, CHUNK), pl.ds(column, width)
        ]

    def place_copy(chunk):
        return pltpu.make_async_copy(
            ordered[chunk].at[pl.ds(me * capacity, capacity)], place(chunk), place_sem.at[chunk]
        )

    def dp_copy(chunk, step):
        return pltpu.make_async_remote_copy(
            src_ref=ordered[chunk].at[pl.ds(dp_peer(step) * capacity, capacity)],
            dst_ref=place(chunk),
            send_sem=dp_send.at[chunk, step],
            recv_sem=dp_recv.at[chunk, step],
            device_id={"dp": dp_peer(step)},
            device_id_type=pl.DeviceIdType.MESH,
        )

    def att_copy(step):
        return pltpu.make_async_remote_copy(
            src_ref=partial.at[dp_peer(step)],
            dst_ref=gathered.at[me],
            send_sem=att_send.at[step],
            recv_sem=att_recv.at[step],
            device_id={"dp": dp_peer(step)},
            device_id_type=pl.DeviceIdType.MESH,
        )

    def reduce_copy(step):
        return pltpu.make_async_remote_copy(
            src_ref=outgoing.at[tensor_peer(step)],
            dst_ref=arrived.at[mine],
            send_sem=reduce_send.at[step],
            recv_sem=reduce_recv.at[step],
            device_id={"tensor": tensor_peer(step)},
            device_id_type=pl.DeviceIdType.MESH,
        )

    def share_copy(step):
        return pltpu.make_async_remote_copy(
            src_ref=total,
            dst_ref=attention.at[mine],
            send_sem=share_send.at[step],
            recv_sem=share_recv.at[step],
            device_id={"tensor": tensor_peer(step)},
            device_id_type=pl.DeviceIdType.MESH,
        )

    def start_reduce():
        att_own.wait()
        lax.fori_loop(1, dp_count, lambda step, _: (att_copy(step).wait(), None)[1], None)
        for owner in range(tensor_count):
            rows = gathered[owner * share : (owner + 1) * share]
            outgoing[owner] = rows.reshape(outgoing.shape[1:]).astype(outgoing.dtype)
        for step in range(1, tensor_count):
            reduce_copy(step).start()

    def start_share():
        for step in range(1, tensor_count):
            reduce_copy(step).wait()
        value = outgoing[mine].astype(jnp.float32)
        for step in range(1, tensor_count):
            value += arrived[tensor_peer(step)].astype(jnp.float32)
        total[...] = value.astype(total.dtype)
        for step in range(1, tensor_count):
            share_copy(step).start()
        share_own.start()

    def start_tensor(chunk):
        for step in range(1, tensor_count):
            tensor_copy(chunk, step).start()
        own_copy(chunk).start()

    barrier = pltpu.get_barrier_semaphore()
    for step in range(1, dp_count):
        pl.semaphore_signal(
            barrier, inc=1, device_id={"dp": dp_peer(step)}, device_id_type=pl.DeviceIdType.MESH
        )
    for step in range(1, tensor_count):
        pl.semaphore_signal(
            barrier,
            inc=1,
            device_id={"tensor": tensor_peer(step)},
            device_id_type=pl.DeviceIdType.MESH,
        )
    pl.semaphore_wait(barrier, dp_count - 1 + tensor_count - 1)

    for chunk in range(early_chunks, min(early_chunks + AHEAD, chunks)):
        start_tensor(chunk)
    for chunk in range(early_chunks):
        early_copy(chunk).start()
    att_own = pltpu.make_async_copy(partial.at[me], gathered.at[me], att_sem)
    share_own = pltpu.make_async_copy(total, attention.at[mine], share_sem)
    att_own.start()
    lax.fori_loop(1, dp_count, lambda step, _: (att_copy(step).start(), None)[1], None)

    for chunk in range(chunks):
        if chunk == early_chunks:
            start_reduce()
        if chunk == early_chunks + AHEAD:
            start_share()
        if chunk < early_chunks:
            early_copy(chunk).wait()
        else:
            own_copy(chunk).wait()
            for step in range(1, tensor_count):
                tensor_copy(chunk, step).wait_recv()
            if chunk + AHEAD < chunks:
                start_tensor(chunk + AHEAD)

        def reorder(slot, _, chunk=chunk):
            ordered[chunk][slot] = held[chunk][send_index[slot]]

        lax.fori_loop(0, dp_count * capacity, reorder, None)
        lax.fori_loop(
            1, dp_count, lambda step, _, chunk=chunk: (dp_copy(chunk, step).start(), None)[1], None
        )
        place_copy(chunk).start()

    share_own.wait()
    for step in range(1, tensor_count):
        share_copy(step).wait()
    for chunk in range(chunks):
        if chunk >= early_chunks:
            for step in range(1, tensor_count):
                tensor_copy(chunk, step).wait_send()
        place_copy(chunk).wait()
        lax.fori_loop(
            1, dp_count, lambda step, _, chunk=chunk: (dp_copy(chunk, step).wait(), None)[1], None
        )


def route(send_index, source, early, partial, dp_count, tensor_count, capacity):
    blocks, block_rows, width = source.shape
    group_size = blocks * tensor_count
    columns = width // tensor_count
    parts, early_chunks = chunk_list(block_rows, early.shape[1], columns)
    chunks = len(parts)
    late = chunks - early_chunks
    slots = dp_count * capacity
    shared = (dp_count // tensor_count * partial.shape[1], partial.shape[2])
    exchanged = (tensor_count, *shared)
    anywhere = pl.BlockSpec(memory_space=pl.ANY)
    dma = pltpu.SemaphoreType.DMA
    return pl.pallas_call(
        functools.partial(route_kernel, dp_count, tensor_count),
        out_shape=(
            jax.ShapeDtypeStruct((slots, block_rows, columns), jnp.bfloat16),
            jax.ShapeDtypeStruct(exchanged, jnp.bfloat16),
        ),
        in_specs=[pl.BlockSpec(memory_space=pltpu.SMEM), anywhere, anywhere, anywhere],
        out_specs=(anywhere, anywhere),
        scratch_shapes=[
            pltpu.VMEM((group_size, CHUNK, part[2]), jnp.bfloat16) for part in parts
        ]
        + [pltpu.VMEM((slots, CHUNK, part[2]), jnp.bfloat16) for part in parts]
        + [
            pltpu.VMEM(partial.shape, jnp.float32),
            pltpu.VMEM(exchanged, jnp.bfloat16),
            pltpu.VMEM(exchanged, jnp.bfloat16),
            pltpu.VMEM(shared, jnp.bfloat16),
            dma((early_chunks,)),
            dma((late,)),
            dma((late, tensor_count)),
            dma((late, tensor_count)),
            dma((chunks,)),
            dma((chunks, dp_count)),
            dma((chunks, dp_count)),
            dma,
            dma((dp_count,)),
            dma((dp_count,)),
            dma((tensor_count,)),
            dma((tensor_count,)),
            dma,
            dma((tensor_count,)),
            dma((tensor_count,)),
        ],
        compiler_params=pltpu.CompilerParams(
            collective_id=0, has_side_effects=True, vmem_limit_bytes=44 * 1024 * 1024
        ),
        cost_estimate=pl.CostEstimate(
            flops=0, bytes_accessed=4 * slots * block_rows * columns, transcendentals=0
        ),
        name="route",
    )(send_index, source, early, partial)


def put_kernel(slot_of, incoming, out, held, read_sem, write_sem):
    places = held.shape[0]

    def read(place):
        return pltpu.make_async_copy(
            incoming.at[slot_of[place]], held.at[place], read_sem.at[place]
        )

    def write(place):
        return pltpu.make_async_copy(held.at[place], out.at[place], write_sem.at[place])

    for place in range(places):
        read(place).start()
    for place in range(places):
        read(place).wait()
        write(place).start()
    for place in range(places):
        write(place).wait()


def put(slot_of, incoming):
    group_size = slot_of.shape[0]
    shape = (group_size, *incoming.shape[1:])
    return pl.pallas_call(
        put_kernel,
        out_shape=jax.ShapeDtypeStruct(shape, jnp.bfloat16),
        in_specs=[
            pl.BlockSpec(memory_space=pltpu.SMEM),
            pl.BlockSpec(memory_space=pl.ANY),
        ],
        out_specs=pl.BlockSpec(memory_space=pl.ANY),
        scratch_shapes=[
            pltpu.VMEM(shape, jnp.bfloat16),
            pltpu.SemaphoreType.DMA((group_size,)),
            pltpu.SemaphoreType.DMA((group_size,)),
        ],
        compiler_params=pltpu.CompilerParams(vmem_limit_bytes=56 * 1024 * 1024),
        name="put",
    )(slot_of, incoming)


def routing_tables(block_ids, dp_count):
    group_size = block_ids.shape[0]
    capacity = max(1, group_size // dp_count)
    me = lax.axis_index("dp")
    numbers = lax.all_gather(block_ids, "dp", axis=0)
    target = numbers // group_size
    earlier = jnp.arange(group_size)[:, None] > jnp.arange(group_size)[None, :]
    same = (target[:, :, None] == target[:, None, :]) & earlier[None]
    arrival = jnp.sum(same.astype(jnp.int32), axis=2)
    my_slot = (target * capacity + arrival)[me]
    slots = jnp.arange(dp_count * capacity, dtype=jnp.int32)
    order = jnp.arange(group_size, dtype=jnp.int32)
    send_index = jnp.sum(
        jnp.where(slots[:, None] == my_slot[None, :], order[None, :], 0), axis=1, dtype=jnp.int32
    )
    from_slot = jnp.arange(dp_count, dtype=jnp.int32)[:, None] * capacity + arrival
    wanted = numbers.reshape(-1)[None, :] == (me * group_size + order)[:, None]
    slot_of = jnp.sum(
        jnp.where(wanted, from_slot.reshape(-1)[None, :], 0), axis=1, dtype=jnp.int32
    )
    return send_index, slot_of, capacity


def on_device(
    hidden,
    norm_gain,
    query_weight,
    keyval_weight,
    output_weight,
    kv_cache,
    cache_lengths,
    next_source,
    block_ids,
):
    rows_dev = hidden.shape[0]
    dp_count = lax.axis_size("dp")
    tensor_count = lax.axis_size("tensor")
    blocks, _, width = next_source.shape
    early = lax.all_to_all(
        next_source[:, :EARLY]
        .reshape(blocks, EARLY, tensor_count, width // tensor_count)
        .transpose(2, 0, 1, 3),
        "tensor",
        split_axis=0,
        concat_axis=0,
        tiled=True,
    ).reshape(tensor_count * blocks, EARLY, width // tensor_count)
    send_index, slot_of, capacity = routing_tables(block_ids, dp_count)
    stream = hidden.astype(jnp.float32)
    meansq = jnp.mean(stream * stream, axis=-1, keepdims=True)
    normed = (stream * lax.rsqrt(meansq + 1e-05) * norm_gain.astype(jnp.float32)).astype(
        jnp.bfloat16
    )
    pieces = lax.all_to_all(normed, "dp", split_axis=1, concat_axis=0, tiled=True)
    flat_kv = keyval_weight.reshape(keyval_weight.shape[0], -1)
    query_cols = query_weight.shape[1]
    projected = lax.psum_scatter(
        jnp.concatenate(
            [
                jnp.dot(pieces, query_weight, preferred_element_type=jnp.float32),
                jnp.dot(pieces, flat_kv, preferred_element_type=jnp.float32),
            ],
            axis=1,
        ).astype(jnp.bfloat16),
        "dp",
        scatter_dimension=0,
        tiled=True,
    ).astype(jnp.float32)
    queries = projected[:, :query_cols].astype(jnp.bfloat16)
    new_keyval = (
        projected[:, query_cols:]
        .astype(jnp.bfloat16)
        .reshape(rows_dev, keyval_weight.shape[1], keyval_weight.shape[2])
    )
    heads_out = attend(queries, new_keyval, kv_cache, cache_lengths)
    partial_out = jnp.dot(
        lax.all_gather(heads_out, "dp", axis=0, tiled=True),
        output_weight,
        preferred_element_type=jnp.float32,
    )
    incoming, attention = route(
        send_index,
        next_source,
        early,
        partial_out.reshape(dp_count, rows_dev, -1),
        dp_count,
        tensor_count,
        capacity,
    )
    next_weight = put(slot_of, incoming).reshape(-1, incoming.shape[2])
    attention = attention.reshape(dp_count, rows_dev, -1).transpose(1, 0, 2)
    attention = attention.reshape(rows_dev, -1).astype(jnp.float32)
    mixed = (stream + attention).astype(jnp.bfloat16)
    return (mixed, next_weight)


def solution(mesh):
    return jax.shard_map(
        on_device,
        mesh=mesh,
        in_specs=(
            P("dp", None),
            P(),
            P("dp", "tensor"),
            P("dp", "tensor", None),
            P("tensor", "dp"),
            P("dp", "tensor", None, None),
            P("dp"),
            P(("dp", "tensor"), None, None),
            P("dp"),
        ),
        out_specs=(P("dp", None), P("dp", "tensor")),
        check_vma=False,
    )
```

```python
import functools

import jax
import jax.numpy as jnp
from jax import lax
from jax.experimental import pallas as pl
from jax.experimental.pallas import tpu as pltpu
from jax.sharding import PartitionSpec as P


def attend(queries, new_keyval, kv_cache, cache_lengths):
    rows, groups, length, twice = kv_cache.shape
    head_dim = twice // 2
    score_scale = head_dim ** (-0.5)
    query_heads = queries.reshape(rows, groups, -1, head_dim)
    scores = (
        jnp.einsum(
            "rjhd,rjpd->rjhp",
            query_heads,
            kv_cache[..., :head_dim],
            preferred_element_type=jnp.float32,
        )
        * score_scale
    )
    visible = jnp.arange(length)[None, :] < cache_lengths[:, None]
    scores = jnp.where(visible[:, None, None, :], scores, -jnp.inf)
    self_score = (
        jnp.einsum(
            "rjhd,rjd->rjh",
            query_heads,
            new_keyval[..., :head_dim],
            preferred_element_type=jnp.float32,
        )
        * score_scale
    )
    highest = jnp.maximum(jnp.max(scores, axis=-1), self_score)
    expo = jnp.exp(scores - highest[..., None])
    self_expo = jnp.exp(self_score - highest)
    denominator = jnp.sum(expo, axis=-1) + self_expo
    weights = (expo / denominator[..., None]).astype(jnp.bfloat16)
    self_weight = (self_expo / denominator).astype(jnp.bfloat16)
    summed = jnp.einsum(
        "rjhp,rjpd->rjhd", weights, kv_cache[..., head_dim:], preferred_element_type=jnp.float32
    )
    summed = summed + self_weight.astype(jnp.float32)[..., None] * new_keyval[
        :, :, None, head_dim:
    ].astype(jnp.float32)
    return summed.astype(jnp.bfloat16).reshape(rows, -1)


CHUNK = 16
EARLY = 32
AHEAD = 3
TAIL_PARTS = 4


def chunk_list(block_rows, early_rows, columns):
    parts = [(row, 0, columns) for row in range(0, block_rows - CHUNK, CHUNK)]
    width = columns // TAIL_PARTS
    parts += [(block_rows - CHUNK, width * part, width) for part in range(TAIL_PARTS)]
    return parts, early_rows // CHUNK


def route_kernel(
    dp_count,
    tensor_count,
    send_index,
    source,
    partial,
    *refs,
):
    early = refs[: tensor_count - 1]
    incoming, attention, *scratch = refs[tensor_count - 1 :]
    blocks, block_rows, _ = source.shape
    columns = incoming.shape[2]
    capacity = incoming.shape[0] // dp_count
    parts, early_chunks = chunk_list(block_rows, early[0].shape[1], columns)
    chunks = len(parts)
    held = scratch[:chunks]
    ordered = scratch[chunks : 2 * chunks]
    (
        gathered,
        outgoing,
        arrived,
        total,
        early_sem,
        own_sem,
        tensor_send,
        tensor_recv,
        place_sem,
        dp_send,
        dp_recv,
        att_sem,
        att_send,
        att_recv,
        reduce_send,
        reduce_recv,
        share_sem,
        share_send,
        share_recv,
    ) = scratch[2 * chunks :]
    share = dp_count // tensor_count
    me = lax.axis_index("dp")
    mine = lax.axis_index("tensor")

    def dp_peer(step):
        return lax.rem(me + step, dp_count)

    def tensor_peer(step):
        return lax.rem(mine + step, tensor_count)

    def tile(chunk, owner):
        row, column, width = parts[chunk]
        return source.at[
            :,
            pl.ds(row, CHUNK),
            pl.ds(pl.multiple_of(owner * columns + column, 128), width),
        ]

    def early_copy(chunk, step):
        owner = lax.rem(mine + tensor_count - step, tensor_count)
        return pltpu.make_async_copy(
            early[step - 1].at[:, pl.ds(parts[chunk][0], CHUNK), :],
            held[chunk].at[pl.ds(owner * blocks, blocks)],
            early_sem.at[chunk, step],
        )

    def own_copy(chunk):
        return pltpu.make_async_copy(
            tile(chunk, mine),
            held[chunk].at[pl.ds(mine * blocks, blocks)],
            own_sem.at[chunk],
        )

    def tensor_copy(chunk, step):
        return pltpu.make_async_remote_copy(
            src_ref=tile(chunk, tensor_peer(step)),
            dst_ref=held[chunk].at[pl.ds(mine * blocks, blocks)],
            send_sem=tensor_send.at[chunk - early_chunks, step],
            recv_sem=tensor_recv.at[chunk - early_chunks, step],
            device_id={"tensor": tensor_peer(step)},
            device_id_type=pl.DeviceIdType.MESH,
        )

    def place(chunk):
        row, column, width = parts[chunk]
        return incoming.at[
            pl.ds(me * capacity, capacity), pl.ds(row, CHUNK), pl.ds(column, width)
        ]

    def place_copy(chunk):
        return pltpu.make_async_copy(
            ordered[chunk].at[pl.ds(me * capacity, capacity)], place(chunk), place_sem.at[chunk]
        )

    def dp_copy(chunk, step):
        return pltpu.make_async_remote_copy(
            src_ref=ordered[chunk].at[pl.ds(dp_peer(step) * capacity, capacity)],
            dst_ref=place(chunk),
            send_sem=dp_send.at[chunk, step],
            recv_sem=dp_recv.at[chunk, step],
            device_id={"dp": dp_peer(step)},
            device_id_type=pl.DeviceIdType.MESH,
        )

    def att_copy(step):
        return pltpu.make_async_remote_copy(
            src_ref=partial.at[dp_peer(step)],
            dst_ref=gathered.at[me],
            send_sem=att_send.at[step],
            recv_sem=att_recv.at[step],
            device_id={"dp": dp_peer(step)},
            device_id_type=pl.DeviceIdType.MESH,
        )

    def reduce_copy(step):
        return pltpu.make_async_remote_copy(
            src_ref=outgoing.at[tensor_peer(step)],
            dst_ref=arrived.at[mine],
            send_sem=reduce_send.at[step],
            recv_sem=reduce_recv.at[step],
            device_id={"tensor": tensor_peer(step)},
            device_id_type=pl.DeviceIdType.MESH,
        )

    def share_copy(step):
        return pltpu.make_async_remote_copy(
            src_ref=total,
            dst_ref=attention.at[mine],
            send_sem=share_send.at[step],
            recv_sem=share_recv.at[step],
            device_id={"tensor": tensor_peer(step)},
            device_id_type=pl.DeviceIdType.MESH,
        )

    def start_reduce():
        att_own.wait()
        lax.fori_loop(1, dp_count, lambda step, _: (att_copy(step).wait(), None)[1], None)
        for owner in range(tensor_count):
            rows = gathered[owner * share : (owner + 1) * share]
            outgoing[owner] = rows.reshape(outgoing.shape[1:]).astype(outgoing.dtype)
        for step in range(1, tensor_count):
            reduce_copy(step).start()

    def start_share():
        for step in range(1, tensor_count):
            reduce_copy(step).wait()
        value = outgoing[mine].astype(jnp.float32)
        for step in range(1, tensor_count):
            value += arrived[tensor_peer(step)].astype(jnp.float32)
        total[...] = value.astype(total.dtype)
        for step in range(1, tensor_count):
            share_copy(step).start()
        share_own.start()

    def start_tensor(chunk):
        for step in range(1, tensor_count):
            tensor_copy(chunk, step).start()
        own_copy(chunk).start()

    barrier = pltpu.get_barrier_semaphore()
    for step in range(1, dp_count):
        pl.semaphore_signal(
            barrier, inc=1, device_id={"dp": dp_peer(step)}, device_id_type=pl.DeviceIdType.MESH
        )
    for step in range(1, tensor_count):
        pl.semaphore_signal(
            barrier,
            inc=1,
            device_id={"tensor": tensor_peer(step)},
            device_id_type=pl.DeviceIdType.MESH,
        )
    pl.semaphore_wait(barrier, dp_count - 1 + tensor_count - 1)

    for chunk in range(early_chunks, min(early_chunks + AHEAD, chunks)):
        start_tensor(chunk)
    for chunk in range(early_chunks):
        own_copy(chunk).start()
        for step in range(1, tensor_count):
            early_copy(chunk, step).start()
    att_own = pltpu.make_async_copy(partial.at[me], gathered.at[me], att_sem)
    share_own = pltpu.make_async_copy(total, attention.at[mine], share_sem)
    att_own.start()
    lax.fori_loop(1, dp_count, lambda step, _: (att_copy(step).start(), None)[1], None)

    for chunk in range(chunks):
        if chunk == early_chunks:
            start_reduce()
        if chunk == early_chunks + AHEAD:
            start_share()
        if chunk < early_chunks:
            own_copy(chunk).wait()
            for step in range(1, tensor_count):
                early_copy(chunk, step).wait()
        else:
            own_copy(chunk).wait()
            for step in range(1, tensor_count):
                tensor_copy(chunk, step).wait_recv()
            if chunk + AHEAD < chunks:
                start_tensor(chunk + AHEAD)

        def reorder(slot, _, chunk=chunk):
            ordered[chunk][slot] = held[chunk][send_index[slot]]

        lax.fori_loop(0, dp_count * capacity, reorder, None)
        lax.fori_loop(
            1, dp_count, lambda step, _, chunk=chunk: (dp_copy(chunk, step).start(), None)[1], None
        )
        place_copy(chunk).start()

    share_own.wait()
    for step in range(1, tensor_count):
        share_copy(step).wait()
    for chunk in range(chunks):
        if chunk >= early_chunks:
            for step in range(1, tensor_count):
                tensor_copy(chunk, step).wait_send()
        place_copy(chunk).wait()
        lax.fori_loop(
            1, dp_count, lambda step, _, chunk=chunk: (dp_copy(chunk, step).wait(), None)[1], None
        )


def route(send_index, source, early, partial, dp_count, tensor_count, capacity):
    blocks, block_rows, width = source.shape
    group_size = blocks * tensor_count
    columns = width // tensor_count
    parts, early_chunks = chunk_list(block_rows, early[0].shape[1], columns)
    chunks = len(parts)
    late = chunks - early_chunks
    slots = dp_count * capacity
    shared = (dp_count // tensor_count * partial.shape[1], partial.shape[2])
    exchanged = (tensor_count, *shared)
    anywhere = pl.BlockSpec(memory_space=pl.ANY)
    dma = pltpu.SemaphoreType.DMA
    return pl.pallas_call(
        functools.partial(route_kernel, dp_count, tensor_count),
        out_shape=(
            jax.ShapeDtypeStruct((slots, block_rows, columns), jnp.bfloat16),
            jax.ShapeDtypeStruct(exchanged, jnp.bfloat16),
        ),
        in_specs=[pl.BlockSpec(memory_space=pltpu.SMEM)] + [anywhere] * (1 + tensor_count),
        out_specs=(anywhere, anywhere),
        scratch_shapes=[
            pltpu.VMEM((group_size, CHUNK, part[2]), jnp.bfloat16) for part in parts
        ]
        + [pltpu.VMEM((slots, CHUNK, part[2]), jnp.bfloat16) for part in parts]
        + [
            pltpu.VMEM(partial.shape, jnp.float32),
            pltpu.VMEM(exchanged, jnp.bfloat16),
            pltpu.VMEM(exchanged, jnp.bfloat16),
            pltpu.VMEM(shared, jnp.bfloat16),
            dma((early_chunks, tensor_count)),
            dma((chunks,)),
            dma((late, tensor_count)),
            dma((late, tensor_count)),
            dma((chunks,)),
            dma((chunks, dp_count)),
            dma((chunks, dp_count)),
            dma,
            dma((dp_count,)),
            dma((dp_count,)),
            dma((tensor_count,)),
            dma((tensor_count,)),
            dma,
            dma((tensor_count,)),
            dma((tensor_count,)),
        ],
        compiler_params=pltpu.CompilerParams(
            collective_id=0, has_side_effects=True, vmem_limit_bytes=44 * 1024 * 1024
        ),
        cost_estimate=pl.CostEstimate(
            flops=0, bytes_accessed=4 * slots * block_rows * columns, transcendentals=0
        ),
        name="route",
    )(send_index, source, partial, *early)


def put_kernel(slot_of, incoming, out, held, read_sem, write_sem):
    places = held.shape[0]

    def read(place):
        return pltpu.make_async_copy(
            incoming.at[slot_of[place]], held.at[place], read_sem.at[place]
        )

    def write(place):
        return pltpu.make_async_copy(held.at[place], out.at[place], write_sem.at[place])

    for place in range(places):
        read(place).start()
    for place in range(places):
        read(place).wait()
        write(place).start()
    for place in range(places):
        write(place).wait()


def put(slot_of, incoming):
    group_size = slot_of.shape[0]
    shape = (group_size, *incoming.shape[1:])
    return pl.pallas_call(
        put_kernel,
        out_shape=jax.ShapeDtypeStruct(shape, jnp.bfloat16),
        in_specs=[
            pl.BlockSpec(memory_space=pltpu.SMEM),
            pl.BlockSpec(memory_space=pl.ANY),
        ],
        out_specs=pl.BlockSpec(memory_space=pl.ANY),
        scratch_shapes=[
            pltpu.VMEM(shape, jnp.bfloat16),
            pltpu.SemaphoreType.DMA((group_size,)),
            pltpu.SemaphoreType.DMA((group_size,)),
        ],
        compiler_params=pltpu.CompilerParams(vmem_limit_bytes=56 * 1024 * 1024),
        name="put",
    )(slot_of, incoming)


def routing_tables(block_ids, dp_count):
    group_size = block_ids.shape[0]
    capacity = max(1, group_size // dp_count)
    me = lax.axis_index("dp")
    numbers = lax.all_gather(block_ids, "dp", axis=0)
    target = numbers // group_size
    earlier = jnp.arange(group_size)[:, None] > jnp.arange(group_size)[None, :]
    same = (target[:, :, None] == target[:, None, :]) & earlier[None]
    arrival = jnp.sum(same.astype(jnp.int32), axis=2)
    my_slot = (target * capacity + arrival)[me]
    slots = jnp.arange(dp_count * capacity, dtype=jnp.int32)
    order = jnp.arange(group_size, dtype=jnp.int32)
    send_index = jnp.sum(
        jnp.where(slots[:, None] == my_slot[None, :], order[None, :], 0), axis=1, dtype=jnp.int32
    )
    from_slot = jnp.arange(dp_count, dtype=jnp.int32)[:, None] * capacity + arrival
    wanted = numbers.reshape(-1)[None, :] == (me * group_size + order)[:, None]
    slot_of = jnp.sum(
        jnp.where(wanted, from_slot.reshape(-1)[None, :], 0), axis=1, dtype=jnp.int32
    )
    return send_index, slot_of, capacity


def on_device(
    hidden,
    norm_gain,
    query_weight,
    keyval_weight,
    output_weight,
    kv_cache,
    cache_lengths,
    next_source,
    block_ids,
):
    rows_dev = hidden.shape[0]
    dp_count = lax.axis_size("dp")
    tensor_count = lax.axis_size("tensor")
    blocks, _, width = next_source.shape
    columns = width // tensor_count
    mine = lax.axis_index("tensor")
    early = [
        lax.ppermute(
            lax.dynamic_slice(
                next_source,
                (0, 0, lax.rem(mine + step, tensor_count) * columns),
                (blocks, EARLY, columns),
            ),
            "tensor",
            [(place, (place + step) % tensor_count) for place in range(tensor_count)],
        )
        for step in range(1, tensor_count)
    ]
    send_index, slot_of, capacity = routing_tables(block_ids, dp_count)
    stream = hidden.astype(jnp.float32)
    meansq = jnp.mean(stream * stream, axis=-1, keepdims=True)
    normed = (stream * lax.rsqrt(meansq + 1e-05) * norm_gain.astype(jnp.float32)).astype(
        jnp.bfloat16
    )
    pieces = lax.all_to_all(normed, "dp", split_axis=1, concat_axis=0, tiled=True)
    flat_kv = keyval_weight.reshape(keyval_weight.shape[0], -1)
    query_cols = query_weight.shape[1]
    projected = lax.psum_scatter(
        jnp.concatenate(
            [
                jnp.dot(pieces, query_weight, preferred_element_type=jnp.float32),
                jnp.dot(pieces, flat_kv, preferred_element_type=jnp.float32),
            ],
            axis=1,
        ).astype(jnp.bfloat16),
        "dp",
        scatter_dimension=0,
        tiled=True,
    ).astype(jnp.float32)
    queries = projected[:, :query_cols].astype(jnp.bfloat16)
    new_keyval = (
        projected[:, query_cols:]
        .astype(jnp.bfloat16)
        .reshape(rows_dev, keyval_weight.shape[1], keyval_weight.shape[2])
    )
    heads_out = attend(queries, new_keyval, kv_cache, cache_lengths)
    partial_out = jnp.dot(
        lax.all_gather(heads_out, "dp", axis=0, tiled=True),
        output_weight,
        preferred_element_type=jnp.float32,
    )
    incoming, attention = route(
        send_index,
        next_source,
        early,
        partial_out.reshape(dp_count, rows_dev, -1),
        dp_count,
        tensor_count,
        capacity,
    )
    next_weight = put(slot_of, incoming).reshape(-1, incoming.shape[2])
    attention = attention.reshape(dp_count, rows_dev, -1).transpose(1, 0, 2)
    attention = attention.reshape(rows_dev, -1).astype(jnp.float32)
    mixed = (stream + attention).astype(jnp.bfloat16)
    return (mixed, next_weight)


def solution(mesh):
    return jax.shard_map(
        on_device,
        mesh=mesh,
        in_specs=(
            P("dp", None),
            P(),
            P("dp", "tensor"),
            P("dp", "tensor", None),
            P("tensor", "dp"),
            P("dp", "tensor", None, None),
            P("dp"),
            P(("dp", "tensor"), None, None),
            P("dp"),
        ),
        out_specs=(P("dp", None), P("dp", "tensor")),
        check_vma=False,
    )
```
